1024 devices in a mesh: tensor: 16 (over x, y), dp: 64 (over z, core).
Axes of the slice: x: 4, y: 4, z: 32, core: 2. Of those that a mesh axis runs over, the one named last changes fastest.
Arguments:
- tokens: bfloat16 [1024, 8192], P('dp', 'tensor'), may hold values from -6 to 6
- pad_mask: int32 [1024], P('dp'), may hold values 0 or 1
- gate_weight: bfloat16 [8192, 28672], P('tensor', 'dp'), may hold values from -0.0625 to 0.0625
- up_weight: bfloat16 [8192, 28672], P('tensor', 'dp'), may hold values from -0.0625 to 0.0625
- down_weight: bfloat16 [28672, 8192], P('dp', 'tensor'), may hold values from -0.03125 to 0.03125
Outputs:
- mixed: bfloat16 [1024, 8192], P('dp', 'tensor')
The draws below stay inside these ranges and needn't reach their ends.
All inputs are finite; a program needn't handle non-finite values. No bound on the sum of `pad_mask` on one device may be relied on, other than what follows from the above.
Results may differ from the reference program's by a relative error of at most 0.028.
Values may be sent and summed in bfloat16 or wider, within the bound.
No kernel may reach another device: no remote copies, remote signals or barrier semaphores. Data moves between devices by JAX's collectives and lax.ppermute only.
A program may use at most 32 MiB of HBM per device.

```python
import jax
import jax.numpy as jnp
from jax import lax

D = 8192
FF = 28672
TOKENS = 1024
N_TENSOR = 16


def plant(values, own_key, low, top_value):
    index_at = [jax.random.randint(jax.random.fold_in(own_key, axis), (), 0, length) for axis, length in enumerate(values.shape)]
    longest = values.shape.index(max(values.shape))
    beside = index_at[:longest] + [(index_at[longest] + 1) % values.shape[longest]] + index_at[longest + 1:]
    return values.at[tuple(index_at)].set(low).at[tuple(beside)].set(top_value)


def levels(key, extent, split, low, top_value):
    def one(dim, blocks):
        steps = jax.random.uniform(jax.random.fold_in(jax.random.fold_in(key, 6), dim), (blocks,), jnp.float32, low / len(split), top_value / len(split))
        return jnp.repeat(jnp.exp(steps), extent[dim] // blocks).reshape((-1,) + (1,) * (len(extent) - dim - 1))

    loudness = one(*split[0])
    for cut in split[1:]:
        loudness = loudness * one(*cut)
    return loudness


def centred(own_key, shape, width, most, split=(), dtype=jnp.bfloat16):
    array = jax.random.normal(own_key, shape, jnp.float32) * width
    if len(split) > 0:
        array = levels(own_key, shape, split, -0.22, 0.18) * array
    return jnp.clip(array, min=-most, max=most).astype(dtype)


def setup_inputs(seed: int = 0) -> dict:
    key_list = jax.random.split(jax.random.key(seed), 6)
    return {
        "tokens": centred(key_list[0], (TOKENS, D), 1.0, 6.0, ((0, 64), (1, 16))),
        "pad_mask": plant((jax.random.randint(key_list[1], (TOKENS,), 0, 4) < 3).astype(jnp.int32), jax.random.fold_in(key_list[1], 1), 0, 1),
        "gate_weight": centred(key_list[2], (D, FF), D ** -0.5, 0.0625, ((0, 16), (1, 64))),
        "up_weight": centred(key_list[3], (D, FF), D ** -0.5, 0.0625, ((0, 16), (1, 64))),
        "down_weight": centred(key_list[4], (FF, D), FF ** -0.5, 0.03125, ((0, 64), (1, 16))),
    }


def reference(tokens, pad_mask, gate_weight, up_weight, down_weight):
    feats = D // N_TENSOR
    gate = jnp.zeros((TOKENS, FF), jnp.float32)
    up = jnp.zeros((TOKENS, FF), jnp.float32)
    for block in range(N_TENSOR):
        lo = block * feats
        rows_in = tokens[:, lo:lo + feats]
        part_gate = jnp.dot(rows_in, gate_weight[lo:lo + feats], preferred_element_type=jnp.float32).astype(jnp.bfloat16)
        part_up = jnp.dot(rows_in, up_weight[lo:lo + feats], preferred_element_type=jnp.float32).astype(jnp.bfloat16)
        part_gate, part_up = lax.optimization_barrier((part_gate, part_up))
        gate = gate + part_gate.astype(jnp.float32)
        up = up + part_up.astype(jnp.float32)
    sigma = jax.nn.sigmoid(gate)
    hidden = (gate * sigma * up).astype(jnp.bfloat16)
    result = jnp.dot(hidden, down_weight, preferred_element_type=jnp.float32)
    return (result * pad_mask[:, None].astype(jnp.float32)).astype(jnp.bfloat16)
```

```python
import jax
import jax.numpy as jnp
from jax import lax
from jax.sharding import Mesh, PartitionSpec as P

X, Y, ZH, ZL, C = 4, 4, 8, 4, 2
DP = ("zh", "zl", "c")
TENSOR = ("x", "y")
F32 = jnp.float32
BF16 = jnp.bfloat16


def exchange(pieces, axes):
    return lax.all_to_all(pieces, axes, split_axis=0, concat_axis=0, tiled=True)


def spread(block, count, axes):
    return exchange(jnp.broadcast_to(block[None], (count,) + block.shape), axes)


def swap_cores(block):
    return lax.ppermute(block, "c", [(0, 1), (1, 0)])


def on_device(tokens, pad_mask, gate_weight, up_weight, down_weight):
    rows, feats = tokens.shape
    width = gate_weight.shape[1]
    sub = rows // X

    far = spread(tokens, ZH, "zh")
    far = far.reshape(ZH, X, sub, feats).transpose(1, 0, 2, 3).reshape(X, 1, ZH * sub, feats)
    far = jnp.broadcast_to(far, (X, ZL, ZH * sub, feats)).reshape(X * ZL, ZH * sub, feats)
    own = exchange(far, ("x", "zl")).reshape(X, ZL, 1, ZH * sub, feats)

    gates = spread(gate_weight, X, "x")
    ups = spread(up_weight, X, "x")
    downs = spread(down_weight, X, "x")

    lhs = jnp.concatenate([own, swap_cores(own)], axis=2)
    count = ZL * C * ZH * sub
    lhs = lhs.reshape(X, count, feats).transpose(1, 0, 2).reshape(count, X * feats)
    gate = jnp.dot(lhs, gates.reshape(X * feats, width), preferred_element_type=F32).astype(BF16)
    up = jnp.dot(lhs, ups.reshape(X * feats, width), preferred_element_type=F32).astype(BF16)
    sums = exchange(jnp.concatenate([gate, up], axis=1).reshape(Y, count // Y, 2 * width), "y")
    sums = jnp.sum(sums.astype(F32), axis=0)
    gate, up = sums[:, :width], sums[:, width:]
    hidden = (gate * jax.nn.sigmoid(gate) * up).astype(BF16)
    hidden = spread(hidden, Y, "y").reshape(count, width)

    part = jnp.einsum("tn,xnf->xtf", hidden, downs, preferred_element_type=F32)
    part = part.reshape(X, ZL, C, ZH * sub, feats)
    other = swap_cores(part[:, :, 1].astype(BF16))
    part = (part[:, :, 0] + other.astype(F32)).astype(BF16)
    part = exchange(part.reshape(X * ZL, ZH * sub, feats), ("x", "zl"))
    part = jnp.sum(part.reshape(X, ZL, ZH * sub, feats).astype(F32), axis=1).astype(BF16)
    part = part.reshape(X, ZH, sub, feats).transpose(1, 0, 2, 3).reshape(ZH, rows, feats)
    result = jnp.sum(exchange(part, "zh").astype(F32), axis=0)
    return (result * pad_mask[:, None].astype(F32)).astype(BF16)


def solution(mesh):
    fine = Mesh(mesh.devices.reshape(X, Y, ZH, ZL, C), TENSOR + DP)
    placed = (P(DP, TENSOR), P(DP), P(TENSOR, DP), P(TENSOR, DP), P(DP, TENSOR))
    return jax.shard_map(
        on_device, mesh=fine, in_specs=placed, out_specs=P(DP, TENSOR), check_vma=False
    )
```

```python
import jax
import jax.numpy as jnp
from jax import lax
from jax.experimental import pallas as pl
from jax.experimental.pallas import tpu as pltpu
from jax.sharding import Mesh, PartitionSpec as P

X, Y, ZH, ZL, C = 4, 4, 8, 4, 2
DP = ("zh", "zl", "c")
TENSOR = ("x", "y")
F32 = jnp.float32
BF16 = jnp.bfloat16
VMEM = pl.BlockSpec(memory_space=pltpu.VMEM)
PARAMS = pltpu.CompilerParams(vmem_limit_bytes=24 << 20)


def exchange(pieces, axes):
    return lax.all_to_all(pieces, axes, split_axis=0, concat_axis=0, tiled=True)


def spread(block, count, axes):
    return exchange(jnp.broadcast_to(block[None], (count,) + block.shape), axes)


def swap_cores(block):
    return lax.ppermute(block, "c", [(0, 1), (1, 0)])


def from_behind(block, step):
    return lax.ppermute(block, "x", [(i, (i + step) % X) for i in range(X)])


def behind(step):
    return lax.rem(lax.axis_index("x") + (X - step), X)


def first_kernel(own_ref, other_ref, *refs):
    weights, out_ref = refs[:-1], refs[-1]
    side, _, rows, columns = out_ref.shape
    total = None
    for step, pair_ref in enumerate(weights):
        block = behind(step)
        pair = pair_ref[...].reshape(columns, pair_ref.shape[2])
        both = jnp.concatenate([own_ref[block], other_ref[block]], axis=0)
        term = lax.dot_general(both, pair, (((1,), (1,)), ((), ())), preferred_element_type=F32)
        total = term if total is None else total + term
    total = total.astype(BF16).reshape(C, side, rows, columns)
    for core in range(C):
        out_ref[:, core] = total[core]


def first(own, other, weights):
    rows = own.shape[1] // ZL
    columns = 2 * weights[0].shape[1]
    return pl.pallas_call(
        first_kernel,
        out_shape=jax.ShapeDtypeStruct((ZL, C, rows, columns), BF16),
        in_specs=[VMEM] * (2 + X),
        out_specs=VMEM,
        compiler_params=PARAMS,
    )(own, other, *weights)


def second_kernel(hidden_ref, *refs):
    weights, own_ref, other_ref = refs[:-2], refs[-2], refs[-1]
    side, rows, width = hidden_ref.shape
    rows = rows // C
    mine = hidden_ref[:, :rows].reshape(side * rows, width)
    other = hidden_ref[:, rows:].reshape(side * rows, width)
    both = jnp.concatenate([mine, other], axis=0)
    for step, down_ref in enumerate(weights):
        part = jnp.dot(both, down_ref[...], preferred_element_type=F32)
        own_ref[behind(step)] = part[: side * rows]
        other_ref[behind(step)] = part[side * rows :].astype(BF16)


def second(hidden, weights):
    shape = (X, hidden.shape[0] * hidden.shape[1] // C, weights[0].shape[1])
    return pl.pallas_call(
        second_kernel,
        out_shape=(jax.ShapeDtypeStruct(shape, F32), jax.ShapeDtypeStruct(shape, BF16)),
        in_specs=[VMEM] * (1 + X),
        out_specs=(VMEM, VMEM),
        compiler_params=PARAMS,
    )(hidden, *weights)


def on_device(tokens, pad_mask, gate_weight, up_weight, down_weight):
    rows, feats = tokens.shape
    width = gate_weight.shape[1]
    sub = rows // X
    some = ZH * sub

    far = spread(tokens, ZH, "zh")
    pair = jnp.stack([gate_weight.T, up_weight.T])
    pairs = [pair, from_behind(pair, 1), None, from_behind(pair, 3)]
    far, pairs[1], pairs[3], down_weight = lax.optimization_barrier((far, pairs[1], pairs[3], down_weight))

    far = far.reshape(ZH, X, sub, feats).transpose(1, 0, 2, 3).reshape(X, 1, some, feats)
    far = jnp.broadcast_to(far, (X, ZL, some, feats)).reshape(X * ZL, some, feats)
    own = exchange(far, ("x", "zl")).reshape(X, ZL * some, feats)
    pairs[2] = from_behind(pair, 2)
    downs = [down_weight] + [from_behind(down_weight, step) for step in range(1, X)]
    own, pairs[2], downs[1] = lax.optimization_barrier((own, pairs[2], downs[1]))

    sums = first(own, swap_cores(own), pairs)
    sums, downs[3] = lax.optimization_barrier((sums, downs[3]))
    sums = exchange(sums.reshape(Y, C * some, 2 * width), "y")
    sums, downs[2] = lax.optimization_barrier((sums, downs[2]))
    sums = jnp.sum(sums.astype(F32), axis=0)
    gate, up = sums[:, :width], sums[:, width:]
    hidden = (gate * jax.nn.sigmoid(gate) * up).astype(BF16)
    hidden = spread(hidden, Y, "y")

    part, other = second(hidden, downs)
    part = (part + swap_cores(other).astype(F32)).astype(BF16)
    part = exchange(part.reshape(X * ZL, some, feats), ("x", "zl"))
    part = jnp.sum(part.reshape(X, ZL, some, feats).astype(F32), axis=1).astype(BF16)
    part = part.reshape(X, ZH, sub, feats).transpose(1, 0, 2, 3).reshape(ZH, rows, feats)
    result = jnp.sum(exchange(part, "zh").astype(F32), axis=0)
    return (result * pad_mask[:, None].astype(F32)).astype(BF16)


def solution(mesh):
    fine = Mesh(mesh.devices.reshape(X, Y, ZH, ZL, C), TENSOR + DP)
    placed = (P(DP, TENSOR), P(DP), P(TENSOR, DP), P(TENSOR, DP), P(DP, TENSOR))
    return jax.shard_map(
        on_device, mesh=fine, in_specs=placed, out_specs=P(DP, TENSOR), check_vma=False
    )
```

```python
import jax
import jax.numpy as jnp
from jax import lax
from jax.experimental import pallas as pl
from jax.experimental.pallas import tpu as pltpu
from jax.sharding import Mesh, PartitionSpec as P

X, Y, ZH, ZL, C = 4, 4, 8, 4, 2
DP = ("zh", "zl", "c")
TENSOR = ("x", "y")
F32 = jnp.float32
BF16 = jnp.bfloat16
STEPS = (0, 1, X - 1, 2)
VMEM = pl.BlockSpec(memory_space=pltpu.VMEM)
PARAMS = pltpu.CompilerParams(vmem_limit_bytes=24 << 20)


def exchange(pieces, axes):
    return lax.all_to_all(pieces, axes, split_axis=0, concat_axis=0, tiled=True)


def spread(block, count, axes):
    return exchange(jnp.broadcast_to(block[None], (count,) + block.shape), axes)


def swap_cores(block):
    return lax.ppermute(block, "c", [(0, 1), (1, 0)])


def from_behind(block, step):
    return lax.ppermute(block, "x", [(i, (i + step) % X) for i in range(X)])


def behind(step):
    return lax.rem(lax.axis_index("x") + (X - step), X)


def first_kernel(own_ref, other_ref, *refs):
    weights, out_ref = refs[:-1], refs[-1]
    side, _, rows, columns = out_ref.shape
    feats = own_ref.shape[3]
    pairs = [ref[...].reshape(columns, feats) for ref in weights[:3]]
    pairs.append(jnp.concatenate([ref[...] for ref in weights[3:]], axis=0))
    total = None
    for step, pair in zip(STEPS, pairs):
        block = behind(step)
        both = [ref[:, block].reshape(side * rows, feats) for ref in (own_ref, other_ref)]
        both = jnp.concatenate(both, axis=0)
        term = lax.dot_general(both, pair, (((1,), (1,)), ((), ())), preferred_element_type=F32)
        total = term if total is None else total + term
    total = total.astype(BF16).reshape(C, side, rows, columns)
    for core in range(C):
        out_ref[:, core] = total[core]


def first(own, other, weights):
    rows = own.shape[2]
    columns = 2 * weights[0].shape[1]
    return pl.pallas_call(
        first_kernel,
        out_shape=jax.ShapeDtypeStruct((ZL, C, rows, columns), BF16),
        in_specs=[VMEM] * (2 + len(weights)),
        out_specs=VMEM,
        compiler_params=PARAMS,
    )(own, other, *weights)


def second_kernel(hidden_ref, *refs):
    weights, own_ref, other_ref = refs[:-2], refs[-2], refs[-1]
    side, rows, width = hidden_ref.shape
    rows = rows // C
    mine = hidden_ref[:, :rows].reshape(side * rows, width)
    other = hidden_ref[:, rows:].reshape(side * rows, width)
    both = jnp.concatenate([mine, other], axis=0)
    downs = [ref[...] for ref in weights[:3]]
    downs.append(jnp.concatenate([ref[...] for ref in weights[3:]], axis=0))
    for step, down in zip(STEPS, downs):
        part = jnp.dot(both, down, preferred_element_type=F32)
        own_ref[behind(step)] = part[: side * rows]
        other_ref[behind(step)] = part[side * rows :].astype(BF16)


def second(hidden, weights):
    shape = (X, hidden.shape[0] * hidden.shape[1] // C, weights[0].shape[1])
    return pl.pallas_call(
        second_kernel,
        out_shape=(jax.ShapeDtypeStruct(shape, F32), jax.ShapeDtypeStruct(shape, BF16)),
        in_specs=[VMEM] * (1 + len(weights)),
        out_specs=(VMEM, VMEM),
        compiler_params=PARAMS,
    )(hidden, *weights)


def on_device(tokens, pad_mask, gate_weight, up_weight, down_weight):
    rows, feats = tokens.shape
    width = gate_weight.shape[1]
    sub = rows // X
    some = ZH * sub
    half = down_weight.shape[0] // 32 * 16

    pair = jnp.stack([gate_weight.T, up_weight.T])
    pairs = [pair, from_behind(pair, 1), from_behind(pair, X - 1)]
    split = exchange(tokens.reshape(X, sub, feats), "x")
    far = spread(split, ZH, "zh")
    pairs += [from_behind(pairs[1][0], 1), from_behind(pairs[2][1], X - 1)]
    far, down_weight, *pairs[3:] = lax.optimization_barrier((far, down_weight, *pairs[3:]))

    far = far.transpose(1, 0, 2, 3).reshape(X, some, feats)
    own = spread(far, ZL, "zl")
    downs = [down_weight, from_behind(down_weight, 1), from_behind(down_weight, X - 1)]
    own, downs[1], downs[2] = lax.optimization_barrier((own, downs[1], downs[2]))
    downs += [from_behind(downs[1][:half], 1), from_behind(downs[2][half:], X - 1)]

    sums = first(own, swap_cores(own), pairs)
    sums = exchange(sums.reshape(Y, C * some, 2 * width), "y")
    sums, *downs[3:] = lax.optimization_barrier((sums, *downs[3:]))
    sums = jnp.sum(sums.astype(F32), axis=0)
    gate, up = sums[:, :width], sums[:, width:]
    hidden = (gate * jax.nn.sigmoid(gate) * up).astype(BF16)
    hidden = spread(hidden, Y, "y")

    part, other = second(hidden, downs)
    part = (part + swap_cores(other).astype(F32)).astype(BF16)
    part = exchange(part.reshape(X * ZL, some, feats), ("x", "zl"))
    part = jnp.sum(part.reshape(X, ZL, some, feats).astype(F32), axis=1).astype(BF16)
    part = part.reshape(X, ZH, sub, feats).transpose(1, 0, 2, 3).reshape(ZH, rows, feats)
    result = jnp.sum(exchange(part, "zh").astype(F32), axis=0)
    return (result * pad_mask[:, None].astype(F32)).astype(BF16)


def solution(mesh):
    fine = Mesh(mesh.devices.reshape(X, Y, ZH, ZL, C), TENSOR + DP)
    placed = (P(DP, TENSOR), P(DP), P(TENSOR, DP), P(TENSOR, DP), P(DP, TENSOR))
    return jax.shard_map(
        on_device, mesh=fine, in_specs=placed, out_specs=P(DP, TENSOR), check_vma=False
    )
```

```python
import jax
import jax.numpy as jnp
from jax import lax
from jax.experimental import pallas as pl
from jax.experimental.pallas import tpu as pltpu
from jax.sharding import Mesh, PartitionSpec as P

XP, XL, Y, ZH, ZL, C = 2, 2, 4, 8, 4, 2
DP = ("zh", "zl", "c")
TENSOR = ("xp", "xl", "y")
F32 = jnp.float32
BF16 = jnp.bfloat16
VMEM = pl.BlockSpec(memory_space=pltpu.VMEM)
PARAMS = pltpu.CompilerParams(vmem_limit_bytes=24 << 20)


def exchange(pieces, axes):
    return lax.all_to_all(pieces, axes, split_axis=0, concat_axis=0, tiled=True)


def spread(block, count, axes):
    return exchange(jnp.broadcast_to(block[None], (count,) + block.shape), axes)


def swap(block, axis):
    return lax.ppermute(block, axis, [(0, 1), (1, 0)])


def first_kernel(tokens_ref, mine, beside, mine_other, beside_other, out_ref):
    feats = tokens_ref.shape[-1]
    place = lax.axis_index("xl")
    here = tokens_ref[place].reshape(-1, feats)
    there = tokens_ref[1 - place].reshape(-1, feats)
    columns = 2 * mine.shape[1]
    for core, (near, far) in enumerate(((mine, beside), (mine_other, beside_other))):
        total = None
        for block, weights in ((here, near), (there, far)):
            pair = weights[:2].reshape(columns, feats)
            term = lax.dot_general(block, pair, (((1,), (1,)), ((), ())), preferred_element_type=F32)
            total = term if total is None else total + term
        out_ref[:, core * columns : (core + 1) * columns] = total.astype(BF16)


def first(tokens, weights):
    rows = tokens.shape[1] * tokens.shape[2]
    return pl.pallas_call(
        first_kernel,
        out_shape=jax.ShapeDtypeStruct((rows, C * 2 * weights[0].shape[1]), BF16),
        in_specs=[VMEM] * (1 + len(weights)),
        out_specs=VMEM,
        compiler_params=PARAMS,
    )(tokens, *weights)


def activate_kernel(sums_ref, out_ref):
    width = out_ref.shape[3]
    sums = jnp.sum(sums_ref[...].astype(F32), axis=0)
    for core in range(C):
        pair = sums[:, core * 2 * width : (core + 1) * 2 * width]
        gate, up = pair[:, :width], pair[:, width:]
        hidden = (gate * jax.nn.sigmoid(gate) * up).astype(BF16)
        for copy in range(out_ref.shape[0]):
            out_ref[copy, core] = hidden


def activate(sums, copies):
    return pl.pallas_call(
        activate_kernel,
        out_shape=jax.ShapeDtypeStruct((copies, C, sums.shape[1], sums.shape[2] // (2 * C)), BF16),
        in_specs=[VMEM],
        out_specs=VMEM,
        compiler_params=PARAMS,
    )(sums)


def second_kernel(hidden_ref, mine, beside, mine_other, beside_other, out_ref):
    width = mine.shape[1]
    place = lax.axis_index("xl")
    hidden = [hidden_ref[:, core].reshape(-1, width) for core in range(C)]
    for block, weights in ((place, (mine, mine_other)), (1 - place, (beside, beside_other))):
        total = None
        for rows, downs in zip(hidden, weights):
            term = jnp.dot(rows, downs[2], preferred_element_type=F32)
            total = term if total is None else total + term
        out_ref[block] = total.astype(BF16)


def second(hidden, weights):
    return pl.pallas_call(
        second_kernel,
        out_shape=jax.ShapeDtypeStruct((XL, hidden.shape[0] * hidden.shape[2], weights[0].shape[2]), BF16),
        in_specs=[VMEM] * (1 + len(weights)),
        out_specs=VMEM,
        compiler_params=PARAMS,
    )(hidden, *weights)


def on_device(tokens, pad_mask, gate_weight, up_weight, down_weight):
    rows, feats = tokens.shape
    width = gate_weight.shape[1]
    sub = rows // XL
    some = ZH * sub

    mine = jnp.stack([gate_weight.T, up_weight.T, down_weight])
    beside = swap(mine, "xl")
    mine_other = swap(mine, "c")
    far = spread(tokens, ZH, "zh")
    far, beside, mine_other = lax.optimization_barrier((far, beside, mine_other))
    beside_other = swap(beside, "c")

    far = far.reshape(ZH, XL, sub, feats).transpose(1, 0, 2, 3).reshape(XL, 1, some, feats)
    far = jnp.broadcast_to(far, (XL, ZL, some, feats)).reshape(XL * ZL, some, feats)
    own = exchange(far, ("xl", "zl")).reshape(XL, ZL, some, feats)
    own, beside_other = lax.optimization_barrier((own, beside_other))
    weights = (mine, beside, mine_other, beside_other)

    groups = XP * Y
    few = ZL * some // groups
    sums = exchange(first(own, weights).reshape(groups, few, C * 2 * width), ("xp", "y"))
    hidden = exchange(activate(sums, groups), ("xp", "y"))

    part = second(hidden, weights).reshape(XL * ZL, some, feats)
    part = exchange(part, ("xl", "zl")).reshape(XL, ZL, some, feats)
    part = jnp.sum(part.astype(F32), axis=1).astype(BF16)
    part = part.reshape(XL, ZH, sub, feats).transpose(1, 0, 2, 3).reshape(ZH, rows, feats)
    result = jnp.sum(exchange(part, "zh").astype(F32), axis=0)
    return (result * pad_mask[:, None].astype(F32)).astype(BF16)


def solution(mesh):
    fine = Mesh(mesh.devices.reshape(XP, XL, Y, ZH, ZL, C), TENSOR + DP)
    placed = (P(DP, TENSOR), P(DP), P(TENSOR, DP), P(TENSOR, DP), P(DP, TENSOR))
    return jax.shard_map(
        on_device, mesh=fine, in_specs=placed, out_specs=P(DP, TENSOR), check_vma=False
    )
```

```python
import jax
import jax.numpy as jnp
from jax import lax
from jax.experimental import pallas as pl
from jax.experimental.pallas import tpu as pltpu
from jax.sharding import Mesh, PartitionSpec as P

XP, XL, Y, ZH, ZL, C = 2, 2, 4, 8, 4, 2
Z = ZH * ZL
DP = ("zh", "zl", "c")
TENSOR = ("xp", "xl", "y")
NEAR = [
    [(xl * Z + (first * ZL + core * ZL // 2 + step) % Z) * C + core for xl in range(XL) for step in range(ZL)]
    for core in range(C)
    for first in range(ZH)
]
F32 = jnp.float32
BF16 = jnp.bfloat16
VMEM = pl.BlockSpec(memory_space=pltpu.VMEM)
PARAMS = pltpu.CompilerParams(vmem_limit_bytes=24 << 20)


def exchange(pieces, axes):
    return lax.all_to_all(pieces, axes, split_axis=0, concat_axis=0, tiled=True)


def near_exchange(pieces):
    return lax.all_to_all(
        pieces, ("xl",) + DP, split_axis=0, concat_axis=0, tiled=True, axis_index_groups=NEAR
    )


def spread(block, count, axes):
    return exchange(jnp.broadcast_to(block[None], (count,) + block.shape), axes)


def swap(block, axis):
    return lax.ppermute(block, axis, [(0, 1), (1, 0)])


def first_kernel(tokens_ref, mine, beside, mine_other, beside_other, out_ref, downs_ref):
    feats = tokens_ref.shape[-1]
    for i, weights in enumerate((mine, beside, mine_other, beside_other)):
        downs_ref[i] = weights[2]
    place = lax.axis_index("xl")
    here = tokens_ref[place].reshape(-1, feats)
    there = tokens_ref[1 - place].reshape(-1, feats)
    columns = 2 * mine.shape[1]
    for core, (near, far) in enumerate(((mine, beside), (mine_other, beside_other))):
        total = None
        for block, weights in ((here, near), (there, far)):
            pair = weights[:2].reshape(columns, feats)
            term = lax.dot_general(block, pair, (((1,), (1,)), ((), ())), preferred_element_type=F32)
            total = term if total is None else total + term
        out_ref[:, core * columns : (core + 1) * columns] = total.astype(BF16)


def first(tokens, weights):
    rows = tokens.shape[1] * tokens.shape[2]
    return pl.pallas_call(
        first_kernel,
        out_shape=(
            jax.ShapeDtypeStruct((rows, C * 2 * weights[0].shape[1]), BF16),
            jax.ShapeDtypeStruct((len(weights),) + weights[0].shape[1:], BF16),
        ),
        in_specs=[VMEM] * (1 + len(weights)),
        out_specs=(VMEM, VMEM),
        compiler_params=PARAMS,
    )(tokens, *weights)


def activate_kernel(sums_ref, out_ref):
    width = out_ref.shape[3]
    sums = jnp.sum(sums_ref[...].astype(F32), axis=0)
    for core in range(C):
        pair = sums[:, core * 2 * width : (core + 1) * 2 * width]
        gate, up = pair[:, :width], pair[:, width:]
        hidden = (gate * jax.nn.sigmoid(gate) * up).astype(BF16)
        for copy in range(out_ref.shape[0]):
            out_ref[copy, core] = hidden


def activate(sums, copies):
    return pl.pallas_call(
        activate_kernel,
        out_shape=jax.ShapeDtypeStruct((copies, C, sums.shape[1], sums.shape[2] // (2 * C)), BF16),
        in_specs=[VMEM],
        out_specs=VMEM,
        compiler_params=PARAMS,
    )(sums)


def second_kernel(hidden_ref, downs_ref, out_ref):
    width = downs_ref.shape[1]
    place = lax.axis_index("xl")
    hidden = [hidden_ref[:, core].reshape(-1, width) for core in range(C)]
    for i, block in enumerate((place, 1 - place)):
        total = None
        for core, rows in enumerate(hidden):
            term = jnp.dot(rows, downs_ref[C * core + i], preferred_element_type=F32)
            total = term if total is None else total + term
        out_ref[block] = total.astype(BF16)


def second(hidden, downs):
    return pl.pallas_call(
        second_kernel,
        out_shape=jax.ShapeDtypeStruct((XL, hidden.shape[0] * hidden.shape[2], downs.shape[2]), BF16),
        in_specs=[VMEM, VMEM],
        out_specs=VMEM,
        compiler_params=PARAMS,
    )(hidden, downs)


def on_device(tokens, pad_mask, gate_weight, up_weight, down_weight):
    rows, feats = tokens.shape
    width = gate_weight.shape[1]
    sub = rows // XL
    some = ZH * sub

    mine = jnp.stack([gate_weight.T, up_weight.T, down_weight])
    beside = swap(mine, "xl")
    far = spread(tokens, ZH, "zh")
    far, beside, mine = lax.optimization_barrier((far, beside, mine))
    mine_other, beside_other = swap(mine, "c"), swap(beside, "c")

    far = far.reshape(ZH, XL, sub, feats).transpose(1, 0, 2, 3).reshape(XL, 1, some, feats)
    far = jnp.broadcast_to(far, (XL, ZL, some, feats)).reshape(XL * ZL, some, feats)
    own = near_exchange(far).reshape(XL, ZL, some, feats)
    weights = (mine, beside, mine_other, beside_other)

    groups = XP * Y
    few = ZL * some // groups
    sums, downs = first(own, weights)
    sums = exchange(sums.reshape(groups, few, C * 2 * width), ("xp", "y"))
    hidden = exchange(activate(sums, groups), ("xp", "y"))

    part = second(hidden, downs).reshape(XL * ZL, some, feats)
    part = near_exchange(part).reshape(XL, ZL, some, feats)
    part = jnp.sum(part.astype(F32), axis=1).astype(BF16)
    part = part.reshape(XL, ZH, sub, feats).transpose(1, 0, 2, 3).reshape(ZH, rows, feats)
    result = jnp.sum(exchange(part, "zh").astype(F32), axis=0)
    return (result * pad_mask[:, None].astype(F32)).astype(BF16)


def solution(mesh):
    fine = Mesh(mesh.devices.reshape(XP, XL, Y, ZH, ZL, C), TENSOR + DP)
    placed = (P(DP, TENSOR), P(DP), P(TENSOR, DP), P(TENSOR, DP), P(DP, TENSOR))
    return jax.shard_map(
        on_device, mesh=fine, in_specs=placed, out_specs=P(DP, TENSOR), check_vma=False
    )
```

```python
import jax
import jax.numpy as jnp
from jax import lax
from jax.experimental import pallas as pl
from jax.experimental.pallas import tpu as pltpu
from jax.sharding import Mesh, PartitionSpec as P

XP, XL, Y, ZH, ZL, C = 2, 2, 4, 8, 4, 2
Z = ZH * ZL
DP = ("zh", "zl", "c")
TENSOR = ("xp", "xl", "y")
NEAR = [
    [(xl * Z + (first * ZL + core * ZL // 2 + step) % Z) * C + core for xl in range(XL) for step in range(ZL)]
    for core in range(C)
    for first in range(ZH)
]
F32 = jnp.float32
BF16 = jnp.bfloat16
VMEM = pl.BlockSpec(memory_space=pltpu.VMEM)
PARAMS = pltpu.CompilerParams(vmem_limit_bytes=24 << 20)


def exchange(pieces, axes):
    return lax.all_to_all(pieces, axes, split_axis=0, concat_axis=0, tiled=True)


def near_exchange(pieces):
    return lax.all_to_all(
        pieces, ("xl",) + DP, split_axis=0, concat_axis=0, tiled=True, axis_index_groups=NEAR
    )


def spread(block, count, axes):
    return exchange(jnp.broadcast_to(block[None], (count,) + block.shape), axes)


def swap(block, axis):
    return lax.ppermute(block, axis, [(0, 1), (1, 0)])


def first_kernel(tokens_ref, *refs):
    weights, out_ref = refs[:-1], refs[-1]
    feats = tokens_ref.shape[-1]
    place = lax.axis_index("xl")
    blocks = [tokens_ref[block].reshape(-1, feats) for block in (place, 1 - place)]
    columns = out_ref.shape[1] // C
    for core in range(C):
        total = None
        for step, block in enumerate(blocks):
            gate_up = weights[4 * core + 2 * step : 4 * core + 2 * step + 2]
            pair = jnp.concatenate([ref[...] for ref in gate_up], axis=0)
            term = lax.dot_general(block, pair, (((1,), (1,)), ((), ())), preferred_element_type=F32)
            total = term if total is None else total + term
        out_ref[:, core * columns : (core + 1) * columns] = total.astype(BF16)


def first(tokens, weights):
    rows = tokens.shape[1] * tokens.shape[2]
    return pl.pallas_call(
        first_kernel,
        out_shape=jax.ShapeDtypeStruct((rows, C * 2 * weights[0].shape[0]), BF16),
        in_specs=[VMEM] * (1 + len(weights)),
        out_specs=VMEM,
        compiler_params=PARAMS,
    )(tokens, *weights)


def activate_kernel(sums_ref, out_ref):
    width = out_ref.shape[3]
    sums = jnp.sum(sums_ref[...].astype(F32), axis=0)
    for core in range(C):
        pair = sums[:, core * 2 * width : (core + 1) * 2 * width]
        gate, up = pair[:, :width], pair[:, width:]
        hidden = (gate * jax.nn.sigmoid(gate) * up).astype(BF16)
        for copy in range(out_ref.shape[0]):
            out_ref[copy, core] = hidden


def activate(sums, copies):
    return pl.pallas_call(
        activate_kernel,
        out_shape=jax.ShapeDtypeStruct((copies, C, sums.shape[1], sums.shape[2] // (2 * C)), BF16),
        in_specs=[VMEM],
        out_specs=VMEM,
        compiler_params=PARAMS,
    )(sums)


def second_kernel(hidden_ref, *refs):
    weights, out_ref = refs[:-1], refs[-1]
    place = lax.axis_index("xl")
    hidden = [hidden_ref[:, core].reshape(-1, hidden_ref.shape[3]) for core in range(C)]
    for step, block in enumerate((place, 1 - place)):
        total = None
        for core, rows in enumerate(hidden):
            term = jnp.dot(rows, weights[C * core + step][...], preferred_element_type=F32)
            total = term if total is None else total + term
        out_ref[block] = total.astype(BF16)


def second(hidden, weights):
    rows = hidden.shape[0] * hidden.shape[2]
    return pl.pallas_call(
        second_kernel,
        out_shape=jax.ShapeDtypeStruct((XL, rows, weights[0].shape[1]), BF16),
        in_specs=[VMEM] * (1 + len(weights)),
        out_specs=VMEM,
        compiler_params=PARAMS,
    )(hidden, *weights)


def near_sum_kernel(parts_ref, out_ref):
    feats = parts_ref.shape[2]
    sums = []
    for xl in range(XL):
        total = jnp.sum(parts_ref[xl * ZL : (xl + 1) * ZL].astype(F32), axis=0)
        sums.append(total.reshape(ZH, -1, feats))
    out_ref[...] = jnp.concatenate(sums, axis=1).astype(BF16)


def near_sum(parts):
    return pl.pallas_call(
        near_sum_kernel,
        out_shape=jax.ShapeDtypeStruct((ZH, XL * parts.shape[1] // ZH, parts.shape[2]), BF16),
        in_specs=[VMEM],
        out_specs=VMEM,
        compiler_params=PARAMS,
    )(parts)


def far_sum_kernel(parts_ref, mask_ref, out_ref):
    total = jnp.sum(parts_ref[...].astype(F32), axis=0)
    out_ref[...] = (total * mask_ref[...].astype(F32)).astype(BF16)


def far_sum(parts, mask):
    return pl.pallas_call(
        far_sum_kernel,
        out_shape=jax.ShapeDtypeStruct(parts.shape[1:], BF16),
        in_specs=[VMEM, VMEM],
        out_specs=VMEM,
        compiler_params=PARAMS,
    )(parts, mask)


def on_device(tokens, pad_mask, gate_weight, up_weight, down_weight):
    rows, feats = tokens.shape
    width = gate_weight.shape[1]
    sub = rows // XL
    some = ZH * sub

    far = spread(tokens, ZH, "zh")
    mine = (gate_weight.T, up_weight.T, down_weight)
    beside = tuple(swap(block, "xl") for block in mine)
    mine_other = tuple(swap(block, "c") for block in mine[:2])
    far, beside, mine_other, down = lax.optimization_barrier((far, beside, mine_other, mine[2]))
    mine_other += (swap(down, "c"),)
    beside_other = tuple(swap(block, "c") for block in beside)
    weights = (mine, beside, mine_other, beside_other)
    gate_ups = [block for blocks in weights for block in blocks[:2]]
    downs = [blocks[2] for blocks in weights]

    far = far.reshape(ZH, XL, sub, feats).transpose(1, 0, 2, 3).reshape(XL, 1, some, feats)
    far = jnp.broadcast_to(far, (XL, ZL, some, feats)).reshape(XL * ZL, some, feats)
    own = near_exchange(far).reshape(XL, ZL, some, feats)

    groups = XP * Y
    few = ZL * some // groups
    sums = first(own, gate_ups)
    sums = exchange(sums.reshape(groups, few, C * 2 * width), ("xp", "y"))
    hidden = exchange(activate(sums, groups), ("xp", "y"))

    part = near_exchange(second(hidden, downs).reshape(XL * ZL, some, feats))
    part = exchange(near_sum(part), "zh")
    return far_sum(part, pad_mask[:, None])


def solution(mesh):
    fine = Mesh(mesh.devices.reshape(XP, XL, Y, ZH, ZL, C), TENSOR + DP)
    placed = (P(DP, TENSOR), P(DP), P(TENSOR, DP), P(TENSOR, DP), P(DP, TENSOR))
    return jax.shard_map(
        on_device, mesh=fine, in_specs=placed, out_specs=P(DP, TENSOR), check_vma=False
    )
```

```python
import jax
import jax.numpy as jnp
from jax import lax
from jax.experimental import pallas as pl
from jax.experimental.pallas import tpu as pltpu
from jax.sharding import Mesh, PartitionSpec as P

XP, XL, Y, ZH, ZL, C = 2, 2, 4, 8, 4, 2
Z = ZH * ZL
DP = ("zh", "zl", "c")
TENSOR = ("xp", "xl", "y")
NEAR = [
    [(xl * Z + (first * ZL + core * ZL // 2 + step) % Z) * C + core for xl in range(XL) for step in range(ZL)]
    for core in range(C)
    for first in range(ZH)
]
F32 = jnp.float32
BF16 = jnp.bfloat16
VMEM = pl.BlockSpec(memory_space=pltpu.VMEM)
PARAMS = pltpu.CompilerParams(vmem_limit_bytes=24 << 20)


def exchange(pieces, axes):
    return lax.all_to_all(pieces, axes, split_axis=0, concat_axis=0, tiled=True)


def near_exchange(pieces):
    return lax.all_to_all(
        pieces, ("xl",) + DP, split_axis=0, concat_axis=0, tiled=True, axis_index_groups=NEAR
    )


def spread(block, count, axes):
    return exchange(jnp.broadcast_to(block[None], (count,) + block.shape), axes)


def swap(block, axis):
    return lax.ppermute(block, axis, [(0, 1), (1, 0)])


def first_kernel(tokens_ref, mine, beside, mine_other, beside_other, out_ref, downs_ref):
    feats = tokens_ref.shape[-1]
    for i, weights in enumerate((mine, beside, mine_other, beside_other)):
        downs_ref[i] = weights[2]
    place = lax.axis_index("xl")
    here = tokens_ref[place].reshape(-1, feats)
    there = tokens_ref[1 - place].reshape(-1, feats)
    columns = 2 * mine.shape[1]
    for core, (near, far) in enumerate(((mine, beside), (mine_other, beside_other))):
        total = None
        for block, weights in ((here, near), (there, far)):
            pair = weights[:2].reshape(columns, feats)
            term = lax.dot_general(block, pair, (((1,), (1,)), ((), ())), preferred_element_type=F32)
            total = term if total is None else total + term
        out_ref[:, core * columns : (core + 1) * columns] = total.astype(BF16)


def first(tokens, weights):
    rows = tokens.shape[1] * tokens.shape[2]
    return pl.pallas_call(
        first_kernel,
        out_shape=(
            jax.ShapeDtypeStruct((rows, C * 2 * weights[0].shape[1]), BF16),
            jax.ShapeDtypeStruct((len(weights),) + weights[0].shape[1:], BF16),
        ),
        in_specs=[VMEM] * (1 + len(weights)),
        out_specs=(VMEM, VMEM),
        compiler_params=PARAMS,
    )(tokens, *weights)


def activate_kernel(sums_ref, out_ref):
    width = out_ref.shape[3]
    sums = jnp.sum(sums_ref[...].astype(F32), axis=0)
    for core in range(C):
        pair = sums[:, core * 2 * width : (core + 1) * 2 * width]
        gate, up = pair[:, :width], pair[:, width:]
        hidden = (gate * jax.nn.sigmoid(gate) * up).astype(BF16)
        for copy in range(out_ref.shape[0]):
            out_ref[copy, core] = hidden


def activate(sums, copies):
    return pl.pallas_call(
        activate_kernel,
        out_shape=jax.ShapeDtypeStruct((copies, C, sums.shape[1], sums.shape[2] // (2 * C)), BF16),
        in_specs=[VMEM],
        out_specs=VMEM,
        compiler_params=PARAMS,
    )(sums)


def second_kernel(hidden_ref, downs_ref, out_ref):
    width = downs_ref.shape[1]
    place = lax.axis_index("xl")
    hidden = [hidden_ref[:, core].reshape(-1, width) for core in range(C)]
    for i, block in enumerate((place, 1 - place)):
        total = None
        for core, rows in enumerate(hidden):
            term = jnp.dot(rows, downs_ref[C * core + i], preferred_element_type=F32)
            total = term if total is None else total + term
        out_ref[block] = total.astype(BF16)


def second(hidden, downs):
    return pl.pallas_call(
        second_kernel,
        out_shape=jax.ShapeDtypeStruct((XL, hidden.shape[0] * hidden.shape[2], downs.shape[2]), BF16),
        in_specs=[VMEM, VMEM],
        out_specs=VMEM,
        compiler_params=PARAMS,
    )(hidden, downs)


def near_sum_kernel(parts_ref, out_ref):
    feats = parts_ref.shape[2]
    sums = []
    for xl in range(XL):
        total = jnp.sum(parts_ref[xl * ZL : (xl + 1) * ZL].astype(F32), axis=0)
        sums.append(total.reshape(ZH, -1, feats))
    out_ref[...] = jnp.concatenate(sums, axis=1).astype(BF16)


def near_sum(parts):
    return pl.pallas_call(
        near_sum_kernel,
        out_shape=jax.ShapeDtypeStruct((ZH, XL * parts.shape[1] // ZH, parts.shape[2]), BF16),
        in_specs=[VMEM],
        out_specs=VMEM,
        compiler_params=PARAMS,
    )(parts)


def far_sum_kernel(parts_ref, mask_ref, out_ref):
    total = jnp.sum(parts_ref[...].astype(F32), axis=0)
    out_ref[...] = (total * mask_ref[...].astype(F32)).astype(BF16)


def far_sum(parts, mask):
    return pl.pallas_call(
        far_sum_kernel,
        out_shape=jax.ShapeDtypeStruct(parts.shape[1:], BF16),
        in_specs=[VMEM, VMEM],
        out_specs=VMEM,
        compiler_params=PARAMS,
    )(parts, mask)


def on_device(tokens, pad_mask, gate_weight, up_weight, down_weight):
    rows, feats = tokens.shape
    width = gate_weight.shape[1]
    sub = rows // XL
    some = ZH * sub

    mine = jnp.stack([gate_weight.T, up_weight.T, down_weight])
    beside = swap(mine, "xl")
    far = spread(tokens, ZH, "zh")
    far, beside, mine = lax.optimization_barrier((far, beside, mine))
    mine_other, beside_other = swap(mine, "c"), swap(beside, "c")

    far = far.reshape(ZH, XL, sub, feats).transpose(1, 0, 2, 3).reshape(XL, 1, some, feats)
    far = jnp.broadcast_to(far, (XL, ZL, some, feats)).reshape(XL * ZL, some, feats)
    own = near_exchange(far).reshape(XL, ZL, some, feats)
    own, mask = lax.optimization_barrier((own, pad_mask[:, None]))
    weights = (mine, beside, mine_other, beside_other)

    groups = XP * Y
    few = ZL * some // groups
    sums, downs = first(own, weights)
    sums = exchange(sums.reshape(groups, few, C * 2 * width), ("xp", "y"))
    hidden = exchange(activate(sums, groups), ("xp", "y"))

    part = near_exchange(second(hidden, downs).reshape(XL * ZL, some, feats))
    part = exchange(near_sum(part), "zh")
    return far_sum(part, mask)


def solution(mesh):
    fine = Mesh(mesh.devices.reshape(XP, XL, Y, ZH, ZL, C), TENSOR + DP)
    placed = (P(DP, TENSOR), P(DP), P(TENSOR, DP), P(TENSOR, DP), P(DP, TENSOR))
    return jax.shard_map(
        on_device, mesh=fine, in_specs=placed, out_specs=P(DP, TENSOR), check_vma=False
    )
```

```python
import jax
import jax.numpy as jnp
from jax import lax
from jax.experimental import pallas as pl
from jax.experimental.pallas import tpu as pltpu
from jax.sharding import Mesh, PartitionSpec as P

XP, XL, Y, ZH, ZL, C = 2, 2, 4, 8, 4, 2
Z = ZH * ZL
DP = ("zh", "zl", "c")
TENSOR = ("xp", "xl", "y")
NEAR = [
    [(xl * Z + (first * ZL + core * ZL // 2 + step) % Z) * C + core for xl in range(XL) for step in range(ZL)]
    for core in range(C)
    for first in range(ZH)
]
F32 = jnp.float32
BF16 = jnp.bfloat16
VMEM = pl.BlockSpec(memory_space=pltpu.VMEM)
PARAMS = pltpu.CompilerParams(vmem_limit_bytes=24 << 20)


def exchange(pieces, axes):
    return lax.all_to_all(pieces, axes, split_axis=0, concat_axis=0, tiled=True)


def near_exchange(pieces):
    return lax.all_to_all(
        pieces, ("xl",) + DP, split_axis=0, concat_axis=0, tiled=True, axis_index_groups=NEAR
    )


def spread(block, count, axes):
    return exchange(jnp.broadcast_to(block[None], (count,) + block.shape), axes)


def swap(block, axis):
    return lax.ppermute(block, axis, [(0, 1), (1, 0)])


def first_kernel(tokens_ref, mine, beside, mine_other, beside_other, out_ref, downs_ref):
    feats = tokens_ref.shape[-1]
    for i, weights in enumerate((mine, beside, mine_other, beside_other)):
        downs_ref[i] = weights[2]
    place = lax.axis_index("xl")
    here = tokens_ref[place].reshape(-1, feats)
    there = tokens_ref[1 - place].reshape(-1, feats)
    columns = 2 * mine.shape[1]
    for core, (near, far) in enumerate(((mine, beside), (mine_other, beside_other))):
        total = None
        for block, weights in ((here, near), (there, far)):
            pair = weights[:2].reshape(columns, feats)
            term = lax.dot_general(block, pair, (((1,), (1,)), ((), ())), preferred_element_type=F32)
            total = term if total is None else total + term
        out_ref[:, core * columns : (core + 1) * columns] = total.astype(BF16)


def first(tokens, weights):
    rows = tokens.shape[1] * tokens.shape[2]
    return pl.pallas_call(
        first_kernel,
        out_shape=(
            jax.ShapeDtypeStruct((rows, C * 2 * weights[0].shape[1]), BF16),
            jax.ShapeDtypeStruct((len(weights),) + weights[0].shape[1:], BF16),
        ),
        in_specs=[VMEM] * (1 + len(weights)),
        out_specs=(VMEM, VMEM),
        compiler_params=PARAMS,
    )(tokens, *weights)


def activate_kernel(sums_ref, out_ref):
    width = out_ref.shape[3]
    sums = jnp.sum(sums_ref[...].astype(F32), axis=0)
    for core in range(C):
        pair = sums[:, core * 2 * width : (core + 1) * 2 * width]
        gate, up = pair[:, :width], pair[:, width:]
        hidden = (gate * jax.nn.sigmoid(gate) * up).astype(BF16)
        for copy in range(out_ref.shape[0]):
            out_ref[copy, core] = hidden


def activate(sums, copies):
    return pl.pallas_call(
        activate_kernel,
        out_shape=jax.ShapeDtypeStruct((copies, C, sums.shape[1], sums.shape[2] // (2 * C)), BF16),
        in_specs=[VMEM],
        out_specs=VMEM,
        compiler_params=PARAMS,
    )(sums)


def second_kernel(hidden_ref, downs_ref, out_ref):
    width = downs_ref.shape[1]
    place = lax.axis_index("xl")
    hidden = [hidden_ref[:, core].reshape(-1, width) for core in range(C)]
    for i, block in enumerate((place, 1 - place)):
        total = None
        for core, rows in enumerate(hidden):
            term = jnp.dot(rows, downs_ref[C * core + i], preferred_element_type=F32)
            total = term if total is None else total + term
        out_ref[block] = total.astype(BF16)


def second(hidden, downs):
    return pl.pallas_call(
        second_kernel,
        out_shape=jax.ShapeDtypeStruct((XL, hidden.shape[0] * hidden.shape[2], downs.shape[2]), BF16),
        in_specs=[VMEM, VMEM],
        out_specs=VMEM,
        compiler_params=PARAMS,
    )(hidden, downs)


def near_sum_kernel(parts_ref, out_ref):
    feats = parts_ref.shape[2]
    sums = []
    for xl in range(XL):
        total = jnp.sum(parts_ref[xl * ZL : (xl + 1) * ZL].astype(F32), axis=0)
        sums.append(total.reshape(ZH, -1, feats))
    out_ref[...] = jnp.concatenate(sums, axis=1).astype(BF16)


def near_sum(parts):
    return pl.pallas_call(
        near_sum_kernel,
        out_shape=jax.ShapeDtypeStruct((ZH, XL * parts.shape[1] // ZH, parts.shape[2]), BF16),
        in_specs=[VMEM],
        out_specs=VMEM,
        compiler_params=PARAMS,
    )(parts)


def far_sum_kernel(parts_ref, mask_ref, out_ref):
    total = jnp.sum(parts_ref[...].astype(F32), axis=0)
    row = lax.broadcasted_iota(jnp.int32, (total.shape[0], 1), 0)
    mask = jnp.zeros_like(row)
    for i in range(total.shape[0]):
        mask = jnp.where(row == i, mask_ref[i], mask)
    out_ref[...] = (total * mask.astype(F32)).astype(BF16)


def far_sum(parts, mask):
    return pl.pallas_call(
        far_sum_kernel,
        out_shape=jax.ShapeDtypeStruct(parts.shape[1:], BF16),
        in_specs=[VMEM, pl.BlockSpec(memory_space=pltpu.SMEM)],
        out_specs=VMEM,
        compiler_params=PARAMS,
    )(parts, mask)


def on_device(tokens, pad_mask, gate_weight, up_weight, down_weight):
    rows, feats = tokens.shape
    width = gate_weight.shape[1]
    sub = rows // XL
    some = ZH * sub

    mine = jnp.stack([gate_weight.T, up_weight.T, down_weight])
    beside = swap(mine, "xl")
    far = spread(tokens, ZH, "zh")
    far, beside, mine = lax.optimization_barrier((far, beside, mine))
    mine_other, beside_other = swap(mine, "c"), swap(beside, "c")

    far = far.reshape(ZH, XL, sub, feats).transpose(1, 0, 2, 3).reshape(XL, 1, some, feats)
    far = jnp.broadcast_to(far, (XL, ZL, some, feats)).reshape(XL * ZL, some, feats)
    own = near_exchange(far).reshape(XL, ZL, some, feats)
    own, mask = lax.optimization_barrier((own, pad_mask))
    weights = (mine, beside, mine_other, beside_other)

    groups = XP * Y
    few = ZL * some // groups
    sums, downs = first(own, weights)
    sums = exchange(sums.reshape(groups, few, C * 2 * width), ("xp", "y"))
    hidden = exchange(activate(sums, groups), ("xp", "y"))

    part = near_exchange(second(hidden, downs).reshape(XL * ZL, some, feats))
    part = exchange(near_sum(part), "zh")
    return far_sum(part, mask)


def solution(mesh):
    fine = Mesh(mesh.devices.reshape(XP, XL, Y, ZH, ZL, C), TENSOR + DP)
    placed = (P(DP, TENSOR), P(DP), P(TENSOR, DP), P(TENSOR, DP), P(DP, TENSOR))
    return jax.shard_map(
        on_device, mesh=fine, in_specs=placed, out_specs=P(DP, TENSOR), check_vma=False
    )
```

```python
import jax
import jax.numpy as jnp
from jax import lax
from jax.experimental import pallas as pl
from jax.experimental.pallas import tpu as pltpu
from jax.sharding import Mesh, PartitionSpec as P

XP, XL, Y, ZH, ZL, C = 2, 2, 4, 8, 4, 2
Z = ZH * ZL
DP = ("zh", "zl", "c")
TENSOR = ("xl", "xp", "y")
NEAR = [
    [(xl * Z + (first * ZL + core * ZL // 2 + step) % Z) * C + core for xl in range(XL) for step in range(ZL)]
    for core in range(C)
    for first in range(ZH)
]
F32 = jnp.float32
BF16 = jnp.bfloat16
VMEM = pl.BlockSpec(memory_space=pltpu.VMEM)
PARAMS = pltpu.CompilerParams(vmem_limit_bytes=24 << 20)


def exchange(pieces, axes):
    return lax.all_to_all(pieces, axes, split_axis=0, concat_axis=0, tiled=True)


def near_exchange(pieces):
    return lax.all_to_all(
        pieces, ("xl",) + DP, split_axis=0, concat_axis=0, tiled=True, axis_index_groups=NEAR
    )


def spread(block, count, axes):
    return exchange(jnp.broadcast_to(block[None], (count,) + block.shape), axes)


def swap(block, axis):
    return lax.ppermute(block, axis, [(0, 1), (1, 0)])


def first_kernel(tokens_ref, mine, beside, mine_other, beside_other, out_ref, downs_ref):
    feats = tokens_ref.shape[-1]
    for i, weights in enumerate((mine, beside, mine_other, beside_other)):
        downs_ref[i] = weights[2]
    place = lax.axis_index("xl")
    here = tokens_ref[place].reshape(-1, feats)
    there = tokens_ref[1 - place].reshape(-1, feats)
    columns = 2 * mine.shape[1]
    for core, (near, far) in enumerate(((mine, beside), (mine_other, beside_other))):
        total = None
        for block, weights in ((here, near), (there, far)):
            pair = weights[:2].reshape(columns, feats)
            term = lax.dot_general(block, pair, (((1,), (1,)), ((), ())), preferred_element_type=F32)
            total = term if total is None else total + term
        out_ref[:, core * columns : (core + 1) * columns] = total.astype(BF16)


def first(tokens, weights):
    rows = tokens.shape[1] * tokens.shape[2]
    return pl.pallas_call(
        first_kernel,
        out_shape=(
            jax.ShapeDtypeStruct((rows, C * 2 * weights[0].shape[1]), BF16),
            jax.ShapeDtypeStruct((len(weights),) + weights[0].shape[1:], BF16),
        ),
        in_specs=[VMEM] * (1 + len(weights)),
        out_specs=(VMEM, VMEM),
        compiler_params=PARAMS,
    )(tokens, *weights)


def activate_kernel(sums_ref, out_ref):
    width = out_ref.shape[3]
    sums = jnp.sum(sums_ref[...].astype(F32), axis=0)
    for core in range(C):
        pair = sums[:, core * 2 * width : (core + 1) * 2 * width]
        gate, up = pair[:, :width], pair[:, width:]
        hidden = (gate * jax.nn.sigmoid(gate) * up).astype(BF16)
        for copy in range(out_ref.shape[0]):
            out_ref[copy, core] = hidden


def activate(sums, copies):
    return pl.pallas_call(
        activate_kernel,
        out_shape=jax.ShapeDtypeStruct((copies, C, sums.shape[1], sums.shape[2] // (2 * C)), BF16),
        in_specs=[VMEM],
        out_specs=VMEM,
        compiler_params=PARAMS,
    )(sums)


def second_kernel(hidden_ref, downs_ref, out_ref):
    width = downs_ref.shape[1]
    place = lax.axis_index("xl")
    hidden = [hidden_ref[:, core].reshape(-1, width) for core in range(C)]
    for i, block in enumerate((place, 1 - place)):
        total = None
        for core, rows in enumerate(hidden):
            term = jnp.dot(rows, downs_ref[C * core + i], preferred_element_type=F32)
            total = term if total is None else total + term
        out_ref[block] = total.astype(BF16)


def second(hidden, downs):
    return pl.pallas_call(
        second_kernel,
        out_shape=jax.ShapeDtypeStruct((XL, hidden.shape[0] * hidden.shape[2], downs.shape[2]), BF16),
        in_specs=[VMEM, VMEM],
        out_specs=VMEM,
        compiler_params=PARAMS,
    )(hidden, downs)


def near_sum_kernel(parts_ref, out_ref):
    feats = parts_ref.shape[2]
    sums = []
    for xl in range(XL):
        total = jnp.sum(parts_ref[xl * ZL : (xl + 1) * ZL].astype(F32), axis=0)
        sums.append(total.reshape(ZH, -1, feats))
    out_ref[...] = jnp.concatenate(sums, axis=1).astype(BF16)


def near_sum(parts):
    return pl.pallas_call(
        near_sum_kernel,
        out_shape=jax.ShapeDtypeStruct((ZH, XL * parts.shape[1] // ZH, parts.shape[2]), BF16),
        in_specs=[VMEM],
        out_specs=VMEM,
        compiler_params=PARAMS,
    )(parts)


def far_sum_kernel(parts_ref, mask_ref, out_ref):
    total = jnp.sum(parts_ref[...].astype(F32), axis=0)
    row = lax.broadcasted_iota(jnp.int32, (total.shape[0], 1), 0)
    mask = jnp.zeros_like(row)
    for i in range(total.shape[0]):
        mask = jnp.where(row == i, mask_ref[i], mask)
    out_ref[...] = (total * mask.astype(F32)).astype(BF16)


def far_sum(parts, mask):
    return pl.pallas_call(
        far_sum_kernel,
        out_shape=jax.ShapeDtypeStruct(parts.shape[1:], BF16),
        in_specs=[VMEM, pl.BlockSpec(memory_space=pltpu.SMEM)],
        out_specs=VMEM,
        compiler_params=PARAMS,
    )(parts, mask)


def on_device(tokens, pad_mask, gate_weight, up_weight, down_weight):
    rows, feats = tokens.shape
    width = gate_weight.shape[1]
    sub = rows // XL
    some = ZH * sub

    mine = jnp.stack([gate_weight.T, up_weight.T, down_weight])
    beside = swap(mine, "xl")
    far = spread(tokens, ZH, "zh")
    far, beside, mine = lax.optimization_barrier((far, beside, mine))
    mine_other, beside_other = swap(mine, "c"), swap(beside, "c")

    far = far.reshape(ZH, XL, sub, feats).transpose(1, 0, 2, 3).reshape(XL, 1, some, feats)
    far = jnp.broadcast_to(far, (XL, ZL, some, feats)).reshape(XL * ZL, some, feats)
    own = near_exchange(far).reshape(XL, ZL, some, feats)
    own, mask = lax.optimization_barrier((own, pad_mask))
    weights = (mine, beside, mine_other, beside_other)

    groups = XP * Y
    few = ZL * some // groups
    sums, downs = first(own, weights)
    sums = exchange(sums.reshape(groups, few, C * 2 * width), ("xp", "y"))
    hidden = exchange(activate(sums, groups), ("xp", "y"))

    part = near_exchange(second(hidden, downs).reshape(XL * ZL, some, feats))
    part = exchange(near_sum(part), "zh")
    return far_sum(part, mask)


def solution(mesh):
    fine = Mesh(mesh.devices.reshape(XL, XP, Y, ZH, ZL, C), TENSOR + DP)
    placed = (P(DP, TENSOR), P(DP), P(TENSOR, DP), P(TENSOR, DP), P(DP, TENSOR))
    return jax.shard_map(
        on_device, mesh=fine, in_specs=placed, out_specs=P(DP, TENSOR), check_vma=False
    )
```
